32 devices in a mesh: group: 2 (over y), latent: 8 (over z, x), dp: 2 (over core).
Axes of the slice: x: 2, y: 2, z: 4, core: 2. Of those that a mesh axis runs over, the one named last changes fastest.
Arguments:
- tokens: bfloat16 [128, 4096], P(('group', 'latent', 'dp')), parts along dimension 0, may hold values from -6 to 6
- enc_weight: bfloat16 [8192, 1024], P('group', 'latent'), parts along dimension 0, may hold values from -0.09375 to 0.09375
- enc_bias: float32 [2048], P(('group', 'latent')), parts along dimension 0, may hold values from -1 to 0.25
- dec_weight: bfloat16 [2048, 4096], P(('group', 'latent')), parts along dimension 0, may hold values from -0.1875 to 0.1875
- dec_bias: float32 [8192], P('group'), parts along dimension 0, may hold values from -3 to 3
Outputs:
- reconstruction: float32 [128, 4096], P(('group', 'latent', 'dp')), parts along dimension 0
- new_enc_weight: bfloat16 [8192, 1024], P('group', 'latent'), parts along dimension 0
- new_enc_bias: float32 [2048], P(('group', 'latent')), parts along dimension 0
- new_dec_weight: bfloat16 [2048, 4096], P(('group', 'latent')), parts along dimension 0
- new_dec_bias: float32 [8192], P('group'), parts along dimension 0
The draws below stay inside these ranges and needn't reach their ends.
There are 2 independent parts, one for each index of `group`. The reference program is written for one: setup_inputs(seed, part) draws one part's arguments, and reference() takes and returns one part's arrays. A program takes and returns all parts, laid end to end along the dimension named above; each array names one. Nothing has to cross between parts.
All inputs are finite; a program needn't handle non-finite values.
Results may differ from the reference program's by a relative error of at most 0.012.
The reference program's roundings to bfloat16 on the way (of `centered`, `codes`, `recon_error` and `code_grad`) count: a program that leaves them out, or rounds other values in their place, can miss the bound.
Values may be sent and summed in bfloat16 or wider, within the bound.
A program may use at most 64 MiB of HBM per device.

```python
import jax
import jax.numpy as jnp
from jax import lax

D = 4096
TOK_DEV = 4
LATENTS = 1024
TOKENS = 64
N_LATENT = 8
N_DP = 2


def level_of(stream_key, extent, shards, smallest, high):
    def one(dim, blocks):
        steps = jax.random.uniform(jax.random.fold_in(jax.random.fold_in(stream_key, 6), dim), (blocks,), jnp.float32, smallest / len(shards), high / len(shards))
        return jnp.repeat(jnp.exp(steps), extent[dim] // blocks).reshape((-1,) + (1,) * (len(extent) - dim - 1))

    loudness = one(*shards[0])
    for cut in shards[1:]:
        loudness = loudness * one(*cut)
    return loudness


def scatter_about(rng, extent, scale, bound, cuts=(), kind=jnp.bfloat16):
    values = jax.random.normal(rng, extent, jnp.float32) * scale
    if len(cuts) > 0:
        values = level_of(rng, extent, cuts, -0.22, 0.18) * values
    return jnp.clip(values, min=-bound, max=bound).astype(kind)


def setup_inputs(seed: int = 0, part: int = 0) -> dict:
    key_of = jax.random.split(jax.random.key(seed), 6)
    part_splits = jax.random.split(jax.random.fold_in(key_of[5], part), 6)
    return {
        "tokens": scatter_about(part_splits[0], (TOKENS, D), 1.0, 6.0, ((0, 16),)),
        "enc_weight": scatter_about(part_splits[1], (D, LATENTS), D ** -0.5, 0.09375, ((1, 8),)),
        "enc_bias": jnp.clip(-1.0 + 1.25 * jax.random.uniform(part_splits[2], (LATENTS,), jnp.float32) ** level_of(part_splits[2], (LATENTS,), ((0, 8),), -0.2, 0.2), -1.0, 0.25),
        "dec_weight": scatter_about(part_splits[3], (LATENTS, D), LATENTS ** -0.5, 0.1875, ((0, 8),)),
        "dec_bias": scatter_about(part_splits[4], (D,), 0.5, 3.0, (), jnp.float32),
    }


STEP_RATE = 0.1


def to_slabs(values):
    return values.reshape(N_LATENT, N_DP, TOK_DEV, -1).transpose(1, 0, 2, 3).reshape(N_DP, N_LATENT * TOK_DEV, -1)


def slab_sum(left, right):
    total = jnp.zeros((left.shape[2], right.shape[2]), jnp.float32)
    for slab_idx in range(N_DP):
        term = lax.dot_general(left[slab_idx], right[slab_idx], (((0,), (0,)), ((), ())), preferred_element_type=jnp.float32)
        total = total + lax.optimization_barrier(term.astype(jnp.bfloat16)).astype(jnp.float32)
    return total


def reference(tokens, enc_weight, enc_bias, dec_weight, dec_bias):
    tokens_wide = tokens.astype(jnp.float32)
    centered = (tokens_wide - dec_bias).astype(jnp.bfloat16)
    preacts = jnp.dot(centered, enc_weight, preferred_element_type=jnp.float32) + enc_bias
    codes = jnp.maximum(preacts, 0.0).astype(jnp.bfloat16)
    reconstruction = jnp.dot(codes, dec_weight, preferred_element_type=jnp.float32) + dec_bias
    recon_error = (reconstruction - tokens_wide).astype(jnp.bfloat16)
    back = lax.dot_general(recon_error, dec_weight, (((1,), (1,)), ((), ())), preferred_element_type=jnp.float32)
    code_grad = jnp.where(codes > 0, back, 0.0).astype(jnp.bfloat16)
    centered_s = to_slabs(centered)
    codes_s = to_slabs(codes)
    error_s = to_slabs(recon_error)
    grad_s = to_slabs(code_grad)
    grad_enc = slab_sum(centered_s, grad_s)
    grad_dec = slab_sum(codes_s, error_s)
    rate_terms = jnp.sum(grad_s.astype(jnp.float32), axis=1)
    grad_enc_bias = jnp.zeros((rate_terms.shape[1],), jnp.float32)
    for slab_idx in range(N_DP):
        grad_enc_bias = grad_enc_bias + lax.optimization_barrier(rate_terms[slab_idx].astype(jnp.bfloat16)).astype(jnp.float32)
    column_rates = jnp.sum(code_grad.astype(jnp.float32), axis=0)
    grad_dec_bias = jnp.sum(recon_error.astype(jnp.float32), axis=0) - jnp.dot(enc_weight.astype(jnp.float32), column_rates, precision=lax.Precision.HIGHEST)
    factor = STEP_RATE * 2.0 / TOKENS
    new_enc_weight = (enc_weight.astype(jnp.float32) - factor * grad_enc).astype(jnp.bfloat16)
    new_dec_weight = (dec_weight.astype(jnp.float32) - factor * grad_dec).astype(jnp.bfloat16)
    new_enc_bias = enc_bias - factor * grad_enc_bias
    new_dec_bias = dec_bias - factor * grad_dec_bias
    return (reconstruction, new_enc_weight, new_enc_bias, new_dec_weight, new_dec_bias)
```

```python
import functools

import jax
import jax.numpy as jnp
from jax import lax
from jax.experimental import pallas as pl
from jax.experimental.pallas import tpu as pltpu
from jax.sharding import PartitionSpec as P

STEP_RATE = 0.1
MESH = pl.DeviceIdType.MESH
ROWS = 16


def kernel(
    nl, factor,
    tokens, enc_hbm, enc_bias, dec_hbm, dec_bias,
    recon_out, new_enc, new_enc_bias, new_dec, new_dec_bias,
    x_all, err_all, r_send, r_recv, enc_cat, dec_cat, e_cat, g_cat, codes_all,
    tok_f, bias_f, work_f, rates, term_send, term_recv, sems, local,
):
    me = lax.axis_index("latent")
    slab = lax.axis_index("dp")
    t, d = tokens.shape
    chunks = ROWS // t
    width = d // chunks
    lat = enc_bias.shape[1]
    nb = 2 * nl
    mine = slab * nl
    other = (1 - slab) * nl

    loads = []
    for c in range(chunks):
        loads.append(pltpu.make_async_copy(
            enc_hbm.at[pl.ds(c * width, width), :], enc_cat.at[:, pl.ds(c * lat, lat)], local.at[0, c]))
    for c in range(chunks):
        loads.append(pltpu.make_async_copy(
            dec_hbm.at[:, pl.ds(c * width, width)], dec_cat.at[pl.ds(c * lat, lat), :], local.at[1, c]))
    for copy in loads:
        copy.start()

    barrier = pltpu.get_barrier_semaphore()

    @pl.loop(1, nl)
    def _(k):
        pl.semaphore_signal(barrier, inc=1, device_id={"latent": lax.rem(me + k, nl)}, device_id_type=MESH)

    pl.semaphore_signal(barrier, inc=1, device_id={"dp": 1 - slab}, device_id_type=MESH)

    for c in range(chunks):
        tok_f[c * t:(c + 1) * t, :] = tokens[:, c * width:(c + 1) * width].astype(jnp.float32)
        bias_f[c * t:(c + 1) * t, :] = jnp.broadcast_to(dec_bias[:, c * width:(c + 1) * width], (t, width))
    x_all[mine + me] = (tok_f[...] - bias_f[...]).astype(jnp.bfloat16)
    pl.semaphore_wait(barrier, nl)

    def to_peer(src, dst, kind, send, recv, peer):
        return pltpu.make_async_remote_copy(
            src_ref=src, dst_ref=dst, send_sem=sems.at[kind, send], recv_sem=sems.at[kind + 1, recv],
            device_id={"latent": peer}, device_id_type=MESH)

    def to_partner(buf, kind, block):
        return pltpu.make_async_remote_copy(
            src_ref=buf.at[mine + block], dst_ref=buf.at[mine + block],
            send_sem=sems.at[kind, block], recv_sem=sems.at[kind + 1, block],
            device_id={"dp": 1 - slab}, device_id_type=MESH)

    def gather_start(buf, kind):
        @pl.loop(1, nl)
        def _(k):
            to_peer(buf.at[mine + me], buf.at[mine + me], kind, k, me, lax.rem(me + k, nl)).start()

        to_partner(buf, kind + 2, me).start()

    def gather_forward(buf, kind):
        @pl.loop(1, nl)
        def _(k):
            src = lax.rem(me + nl - k, nl)
            to_peer(buf.at[mine + src], buf.at[mine + src], kind, k, src, src).wait_recv()
            to_partner(buf, kind + 2, src).start()

    def gather_other(buf, kind):
        @pl.loop(0, nl)
        def _(j):
            pltpu.make_async_remote_copy(
                src_ref=buf.at[other + j], dst_ref=buf.at[other + j],
                send_sem=sems.at[kind + 2, j], recv_sem=sems.at[kind + 3, j],
                device_id={"dp": 1 - slab}, device_id_type=MESH).wait_recv()

    def gather_end(buf, kind):
        @pl.loop(1, nl)
        def _(k):
            to_peer(buf.at[mine + me], buf.at[mine + me], kind, k, me, lax.rem(me + k, nl)).wait_send()

        @pl.loop(0, nl)
        def _(j):
            to_partner(buf, kind + 2, j).wait_send()

    group = 8
    span = group * ROWS
    chunk_of = lax.rem(lax.broadcasted_iota(jnp.int32, (span, lat), 0), ROWS) // t

    def fold(value):
        picked = value[:, :lat]
        for c in range(1, chunks):
            picked = jnp.where(chunk_of == c, value[:, c * lat:(c + 1) * lat], picked)
        picked = picked.reshape(group, ROWS, lat)
        half = picked[:, :8] + picked[:, 8:]
        shift = 4
        while shift >= t:
            half = half + pltpu.roll(half, shift, 1)
            shift //= 2
        return jnp.concatenate([half, half], axis=1).reshape(span, lat)

    def spread(value, dst, row):
        for c in range(chunks):
            dst[pl.ds(row, span), c * lat:(c + 1) * lat] = jnp.where(chunk_of == c, value, 0.0).astype(jnp.bfloat16)

    def encode(first):
        @pl.loop(0, nl // group)
        def _(g):
            block = first + g * group
            row = pl.multiple_of(block * ROWS, span)
            x = x_all[pl.ds(block, group)].reshape(span, width)
            pre = fold(jnp.dot(x, enc_cat[...], preferred_element_type=jnp.float32)) + enc_bias[...]
            codes = jnp.maximum(pre, 0.0).astype(jnp.bfloat16)
            codes_all[pl.ds(row, span), :] = codes
            spread(codes.astype(jnp.float32), e_cat, row)

    gather_start(x_all, 0)
    for c in range(chunks):
        loads[c].wait()
    gather_forward(x_all, 0)
    encode(mine)
    for c in range(chunks):
        loads[chunks + c].wait()

    @pl.loop(0, nl // group)
    def _(g):
        row = pl.multiple_of((mine + g * group) * ROWS, span)
        part = jnp.dot(e_cat[pl.ds(row, span), :], dec_cat[...], preferred_element_type=jnp.float32)
        r_send[pl.ds(g * group, group)] = part.astype(jnp.bfloat16).reshape(group, ROWS, width)

    @pl.loop(1, nl)
    def _(k):
        peer = lax.rem(me + k, nl)
        to_peer(r_send.at[peer], r_recv.at[me], 4, k, me, peer).start()

    gather_other(x_all, 0)
    encode(other)

    work_f[...] = r_send[me].astype(jnp.float32) + bias_f[...]

    @pl.loop(1, nl)
    def _(k):
        src = lax.rem(me + nl - k, nl)
        to_peer(r_send.at[src], r_recv.at[src], 4, k, src, src).wait_recv()
        work_f[...] += r_recv[src].astype(jnp.float32)

    err_all[mine + me] = (work_f[...] - tok_f[...]).astype(jnp.bfloat16)
    gather_start(err_all, 6)
    for c in range(chunks):
        recon_out[:, c * width:(c + 1) * width] = work_f[c * t:(c + 1) * t, :]
    gather_forward(err_all, 6)

    def backward(first, which):
        rates[which:which + 1, :] = jnp.zeros((1, lat), jnp.float32)

        @pl.loop(0, nl // group)
        def _(g):
            block = first + g * group
            row = pl.multiple_of(block * ROWS, span)
            err = err_all[pl.ds(block, group)].reshape(span, width)
            back = fold(lax.dot_general(
                err, dec_cat[...], (((1,), (1,)), ((), ())), preferred_element_type=jnp.float32))
            kept = codes_all[pl.ds(row, span), :].astype(jnp.float32) > 0
            grad = jnp.where(kept, back, 0.0).astype(jnp.bfloat16).astype(jnp.float32)
            spread(grad, g_cat, row)
            rates[which:which + 1, :] += jnp.sum(jnp.where(chunk_of == 0, grad, 0.0), axis=0, keepdims=True)

    backward(mine, 0)
    gather_other(err_all, 6)
    backward(other, 1)

    rate_0, rate_1 = rates[0:1, :], rates[1:2, :]
    new_enc_bias[...] = enc_bias[...] - factor * (
        rate_0.astype(jnp.bfloat16).astype(jnp.float32) + rate_1.astype(jnp.bfloat16).astype(jnp.float32))
    rate = rate_0 + rate_1
    high = rate.astype(jnp.bfloat16).astype(jnp.float32)
    mid = (rate - high).astype(jnp.bfloat16).astype(jnp.float32)
    low = rate - high - mid
    index = lax.broadcasted_iota(jnp.int32, (16, lat), 0)
    pieces = jnp.where(index == 0, high, jnp.where(index == 1, mid, jnp.where(index == 2, low, 0.0)))
    pieces = pieces.astype(jnp.bfloat16)
    eighth = d // 8
    for c in range(chunks):
        term = jnp.sum(lax.dot_general(
            pieces, enc_cat[:, c * lat:(c + 1) * lat], (((1,), (1,)), ((), ())),
            preferred_element_type=jnp.float32), axis=0, keepdims=True)
        for h in range(8 // chunks):
            r = c * (8 // chunks) + h
            term_send[r:r + 1, :] = term[:, h * eighth:(h + 1) * eighth]

    @pl.loop(1, nl)
    def _(k):
        to_peer(term_send, term_recv.at[me], 10, k, me, lax.rem(me + k, nl)).start()

    depth = 256
    tile = 256

    def over_rows(first, second, shape):
        def piece(row):
            return lax.dot_general(
                first(row), second(row), (((0,), (0,)), ((), ())), preferred_element_type=jnp.float32)

        steps = nb * ROWS // depth
        if steps == 1:
            return piece(0)
        return lax.fori_loop(
            0, steps, lambda i, acc: acc + piece(pl.multiple_of(i * depth, depth)), jnp.zeros(shape, jnp.float32))

    def blocks(buf, row, col):
        return buf[pl.ds(row // ROWS, depth // ROWS), :, pl.ds(col, tile)].reshape(depth, tile)

    @pl.loop(0, width // tile)
    def _(i):
        col = pl.multiple_of(i * tile, tile)
        grad = over_rows(
            lambda row: blocks(x_all, row, col), lambda row: g_cat[pl.ds(row, depth), :], (tile, chunks * lat))
        enc_cat[pl.ds(col, tile), :] = (
            enc_cat[pl.ds(col, tile), :].astype(jnp.float32) - factor * grad).astype(jnp.bfloat16)

    stores = []
    for c in range(chunks):
        copy = pltpu.make_async_copy(
            enc_cat.at[:, pl.ds(c * lat, lat)], new_enc.at[pl.ds(c * width, width), :], local.at[2, c])
        copy.start()
        stores.append(copy)

    @pl.loop(0, width // tile)
    def _(i):
        col = pl.multiple_of(i * tile, tile)
        grad = over_rows(
            lambda row: e_cat[pl.ds(row, depth), :], lambda row: blocks(err_all, row, col), (chunks * lat, tile))
        dec_cat[:, pl.ds(col, tile)] = (
            dec_cat[:, pl.ds(col, tile)].astype(jnp.float32) - factor * grad).astype(jnp.bfloat16)

    for c in range(chunks):
        copy = pltpu.make_async_copy(
            dec_cat.at[pl.ds(c * lat, lat), :], new_dec.at[:, pl.ds(c * width, width)], local.at[3, c])
        copy.start()
        stores.append(copy)

    work_f[...] = err_all[0].astype(jnp.float32)

    @pl.loop(1, nb)
    def _(b):
        work_f[...] += err_all[b].astype(jnp.float32)

    total = term_send[...]

    def add_term(k, total):
        src = lax.rem(me + nl - k, nl)
        to_peer(term_send, term_recv.at[src], 10, k, src, src).wait_recv()
        return total + term_recv[src]

    total = lax.fori_loop(1, nl, add_term, total)
    per = 8 // chunks
    for c in range(chunks):
        sums = jnp.sum(work_f[c * t:(c + 1) * t, :], axis=0, keepdims=True)
        for h in range(per):
            r = c * per + h
            cols = slice(r * eighth, (r + 1) * eighth)
            new_dec_bias[:, cols] = dec_bias[:, cols] - factor * (
                sums[:, h * eighth:(h + 1) * eighth] - total[r:r + 1, :])

    gather_end(x_all, 0)
    gather_end(err_all, 6)

    @pl.loop(1, nl)
    def _(k):
        peer = lax.rem(me + k, nl)
        to_peer(r_send.at[peer], r_recv.at[me], 4, k, me, peer).wait_send()
        to_peer(term_send, term_recv.at[me], 10, k, me, peer).wait_send()

    for copy in stores:
        copy.wait()


def on_device(tokens, enc_weight, enc_bias, dec_weight, dec_bias):
    nl = lax.axis_size("latent")
    t, d = tokens.shape
    lat = enc_weight.shape[1]
    nb = 2 * nl
    chunks = ROWS // t
    width = d // chunks
    factor = STEP_RATE * 2.0 / (t * nb)
    vmem = pl.BlockSpec(memory_space=pltpu.VMEM)
    anywhere = pl.BlockSpec(memory_space=pl.ANY)
    bf16, f32 = jnp.bfloat16, jnp.float32
    out = pl.pallas_call(
        functools.partial(kernel, nl, factor),
        out_shape=(
            jax.ShapeDtypeStruct((t, d), f32),
            jax.ShapeDtypeStruct((d, lat), bf16),
            jax.ShapeDtypeStruct((1, lat), f32),
            jax.ShapeDtypeStruct((lat, d), bf16),
            jax.ShapeDtypeStruct((1, d), f32),
        ),
        in_specs=[vmem, anywhere, vmem, anywhere, vmem],
        out_specs=(vmem, anywhere, vmem, anywhere, vmem),
        scratch_shapes=[
            pltpu.VMEM((nb, ROWS, width), bf16),
            pltpu.VMEM((nb, ROWS, width), bf16),
            pltpu.VMEM((nl, ROWS, width), bf16),
            pltpu.VMEM((nl, ROWS, width), bf16),
            pltpu.VMEM((width, chunks * lat), bf16),
            pltpu.VMEM((chunks * lat, width), bf16),
            pltpu.VMEM((nb * ROWS, chunks * lat), bf16),
            pltpu.VMEM((nb * ROWS, chunks * lat), bf16),
            pltpu.VMEM((nb * ROWS, lat), bf16),
            pltpu.VMEM((ROWS, width), f32),
            pltpu.VMEM((ROWS, width), f32),
            pltpu.VMEM((ROWS, width), f32),
            pltpu.VMEM((8, lat), f32),
            pltpu.VMEM((8, d // 8), f32),
            pltpu.VMEM((nl, 8, d // 8), f32),
            pltpu.SemaphoreType.DMA((12, nl)),
            pltpu.SemaphoreType.DMA((4, chunks)),
        ],
        compiler_params=pltpu.CompilerParams(
            collective_id=0, has_side_effects=True, vmem_limit_bytes=56 * 1024 * 1024),
    )(tokens, enc_weight, enc_bias.reshape(1, lat), dec_weight, dec_bias.reshape(1, d))
    recon, new_enc, new_enc_bias, new_dec, new_dec_bias = out
    return recon, new_enc, new_enc_bias.reshape(lat), new_dec, new_dec_bias.reshape(d)


def solution(mesh):
    specs = (
        P(("group", "latent", "dp"), None),
        P("group", "latent"),
        P(("group", "latent")),
        P(("group", "latent"), None),
        P("group"),
    )
    return jax.shard_map(on_device, mesh=mesh, in_specs=specs, out_specs=specs, check_vma=False)
```

```python
import functools

import jax
import jax.numpy as jnp
from jax import lax
from jax.experimental import pallas as pl
from jax.experimental.pallas import tpu as pltpu
from jax.sharding import PartitionSpec as P

STEP_RATE = 0.1
MESH = pl.DeviceIdType.MESH
ROWS = 16


def kernel(
    nl, factor,
    tokens_hbm, enc_hbm, enc_bias_hbm, dec_hbm, dec_bias_hbm,
    recon_out, new_enc, new_enc_bias, new_dec, new_dec_bias,
    x_all, err_all, r_send, r_recv, enc_cat, dec_cat, e_cat, g_cat, codes_all,
    tok_f, bias_f, work_f, rates, term_send, term_recv, tokens, enc_bias, dec_bias, sems, local, small,
):
    me = lax.axis_index("latent")
    slab = lax.axis_index("dp")
    t, d = tokens.shape
    chunks = ROWS // t
    width = d // chunks
    lat = enc_bias.shape[1]
    nb = 2 * nl
    mine = slab * nl
    other = (1 - slab) * nl

    first_loads = [
        pltpu.make_async_copy(src, dst, small.at[i])
        for i, (src, dst) in enumerate(((tokens_hbm, tokens), (dec_bias_hbm, dec_bias), (enc_bias_hbm, enc_bias)))]
    for copy in first_loads:
        copy.start()
    loads = []
    for c in range(chunks):
        loads.append(pltpu.make_async_copy(
            enc_hbm.at[pl.ds(c * width, width), :], enc_cat.at[:, pl.ds(c * lat, lat)], local.at[0, c]))
    for c in range(chunks):
        loads.append(pltpu.make_async_copy(
            dec_hbm.at[:, pl.ds(c * width, width)], dec_cat.at[pl.ds(c * lat, lat), :], local.at[1, c]))
    for copy in loads:
        copy.start()

    barrier = pltpu.get_barrier_semaphore()

    @pl.loop(1, nl)
    def _(k):
        pl.semaphore_signal(barrier, inc=1, device_id={"latent": lax.rem(me + k, nl)}, device_id_type=MESH)

    pl.semaphore_signal(barrier, inc=1, device_id={"dp": 1 - slab}, device_id_type=MESH)

    for copy in first_loads:
        copy.wait()
    for c in range(chunks):
        tok_f[c * t:(c + 1) * t, :] = tokens[:, c * width:(c + 1) * width].astype(jnp.float32)
        bias_f[c * t:(c + 1) * t, :] = jnp.broadcast_to(dec_bias[:, c * width:(c + 1) * width], (t, width))
    x_all[mine + me] = (tok_f[...] - bias_f[...]).astype(jnp.bfloat16)
    pl.semaphore_wait(barrier, nl)

    def to_peer(src, dst, kind, send, recv, peer):
        return pltpu.make_async_remote_copy(
            src_ref=src, dst_ref=dst, send_sem=sems.at[kind, send], recv_sem=sems.at[kind + 1, recv],
            device_id={"latent": peer}, device_id_type=MESH)

    def to_partner(buf, kind, block):
        return pltpu.make_async_remote_copy(
            src_ref=buf.at[mine + block], dst_ref=buf.at[mine + block],
            send_sem=sems.at[kind, block], recv_sem=sems.at[kind + 1, block],
            device_id={"dp": 1 - slab}, device_id_type=MESH)

    pair = me + 1 - 2 * lax.rem(me, 2)

    def gather_start(buf, kind):
        @pl.loop(1, nl // 2)
        def _(k):
            to_peer(buf.at[mine + me], buf.at[mine + me], kind, k, me, lax.rem(me + 2 * k, nl)).start()

        to_peer(buf.at[mine + me], buf.at[mine + me], kind, 0, me, pair).start()
        to_partner(buf, kind + 2, me).start()

    def gather_forward(buf, kind):
        def arrived(src):
            to_peer(buf.at[mine + src], buf.at[mine + src], kind, 0, src, src).wait_recv()

        @pl.loop(1, nl // 2)
        def _(k):
            src = lax.rem(me + nl - 2 * k, nl)
            arrived(src)
            to_peer(buf.at[mine + src], buf.at[mine + src], kind, nl // 2 + k, src, pair).start()
            to_partner(buf, kind + 2, src).start()

        @pl.loop(0, nl // 2)
        def _(k):
            src = lax.rem(pair + nl - 2 * k, nl)
            arrived(src)
            to_partner(buf, kind + 2, src).start()

    def gather_other(buf, kind):
        @pl.loop(0, nl)
        def _(j):
            pltpu.make_async_remote_copy(
                src_ref=buf.at[other + j], dst_ref=buf.at[other + j],
                send_sem=sems.at[kind + 2, j], recv_sem=sems.at[kind + 3, j],
                device_id={"dp": 1 - slab}, device_id_type=MESH).wait_recv()

    def gather_end(buf, kind):
        @pl.loop(1, nl // 2)
        def _(k):
            to_peer(buf.at[mine + me], buf.at[mine + me], kind, k, me, pair).wait_send()
            to_peer(buf.at[mine + me], buf.at[mine + me], kind, nl // 2 + k, me, pair).wait_send()

        to_peer(buf.at[mine + me], buf.at[mine + me], kind, 0, me, pair).wait_send()

        @pl.loop(0, nl)
        def _(j):
            to_partner(buf, kind + 2, j).wait_send()

    group = 8
    span = group * ROWS
    chunk_of = lax.rem(lax.broadcasted_iota(jnp.int32, (span, lat), 0), ROWS) // t

    def fold(value):
        picked = value[:, :lat]
        for c in range(1, chunks):
            picked = jnp.where(chunk_of == c, value[:, c * lat:(c + 1) * lat], picked)
        picked = picked.reshape(group, ROWS, lat)
        half = picked[:, :8] + picked[:, 8:]
        shift = 4
        while shift >= t:
            half = half + pltpu.roll(half, shift, 1)
            shift //= 2
        return jnp.concatenate([half, half], axis=1).reshape(span, lat)

    def spread(value, dst, row):
        for c in range(chunks):
            dst[pl.ds(row, span), c * lat:(c + 1) * lat] = jnp.where(chunk_of == c, value, 0.0).astype(jnp.bfloat16)

    def encode(first):
        @pl.loop(0, nl // group)
        def _(g):
            block = first + g * group
            row = pl.multiple_of(block * ROWS, span)
            x = x_all[pl.ds(block, group)].reshape(span, width)
            pre = fold(jnp.dot(x, enc_cat[...], preferred_element_type=jnp.float32)) + enc_bias[...]
            codes = jnp.maximum(pre, 0.0).astype(jnp.bfloat16)
            codes_all[pl.ds(row, span), :] = codes
            spread(codes.astype(jnp.float32), e_cat, row)

    gather_start(x_all, 0)
    for c in range(chunks):
        loads[c].wait()
    gather_forward(x_all, 0)
    encode(mine)
    for c in range(chunks):
        loads[chunks + c].wait()

    @pl.loop(0, nl // group)
    def _(g):
        row = pl.multiple_of((mine + g * group) * ROWS, span)
        part = jnp.dot(e_cat[pl.ds(row, span), :], dec_cat[...], preferred_element_type=jnp.float32)
        r_send[pl.ds(g * group, group)] = part.astype(jnp.bfloat16).reshape(group, ROWS, width)

    @pl.loop(1, nl)
    def _(k):
        peer = lax.rem(me + k, nl)
        to_peer(r_send.at[peer], r_recv.at[me], 4, k, me, peer).start()

    gather_other(x_all, 0)
    encode(other)

    work_f[...] = r_send[me].astype(jnp.float32) + bias_f[...]

    @pl.loop(1, nl)
    def _(k):
        src = lax.rem(me + nl - k, nl)
        to_peer(r_send.at[src], r_recv.at[src], 4, k, src, src).wait_recv()
        work_f[...] += r_recv[src].astype(jnp.float32)

    err_all[mine + me] = (work_f[...] - tok_f[...]).astype(jnp.bfloat16)
    gather_start(err_all, 6)
    for c in range(chunks):
        recon_out[:, c * width:(c + 1) * width] = work_f[c * t:(c + 1) * t, :]
    gather_forward(err_all, 6)

    def backward(first, which):
        rates[which:which + 1, :] = jnp.zeros((1, lat), jnp.float32)

        @pl.loop(0, nl // group)
        def _(g):
            block = first + g * group
            row = pl.multiple_of(block * ROWS, span)
            err = err_all[pl.ds(block, group)].reshape(span, width)
            back = fold(lax.dot_general(
                err, dec_cat[...], (((1,), (1,)), ((), ())), preferred_element_type=jnp.float32))
            kept = codes_all[pl.ds(row, span), :].astype(jnp.float32) > 0
            grad = jnp.where(kept, back, 0.0).astype(jnp.bfloat16).astype(jnp.float32)
            spread(grad, g_cat, row)
            rates[which:which + 1, :] += jnp.sum(jnp.where(chunk_of == 0, grad, 0.0), axis=0, keepdims=True)

    backward(mine, 0)
    gather_other(err_all, 6)
    backward(other, 1)

    rate_0, rate_1 = rates[0:1, :], rates[1:2, :]
    new_enc_bias[...] = enc_bias[...] - factor * (
        rate_0.astype(jnp.bfloat16).astype(jnp.float32) + rate_1.astype(jnp.bfloat16).astype(jnp.float32))
    rate = rate_0 + rate_1
    high = rate.astype(jnp.bfloat16).astype(jnp.float32)
    mid = (rate - high).astype(jnp.bfloat16).astype(jnp.float32)
    low = rate - high - mid
    index = lax.broadcasted_iota(jnp.int32, (16, lat), 0)
    pieces = jnp.where(index == 0, high, jnp.where(index == 1, mid, jnp.where(index == 2, low, 0.0)))
    pieces = pieces.astype(jnp.bfloat16)
    eighth = d // 8
    for c in range(chunks):
        term = jnp.sum(lax.dot_general(
            pieces, enc_cat[:, c * lat:(c + 1) * lat], (((1,), (1,)), ((), ())),
            preferred_element_type=jnp.float32), axis=0, keepdims=True)
        for h in range(8 // chunks):
            r = c * (8 // chunks) + h
            term_send[r:r + 1, :] = term[:, h * eighth:(h + 1) * eighth]

    @pl.loop(1, nl)
    def _(k):
        to_peer(term_send, term_recv.at[me], 10, k, me, lax.rem(me + k, nl)).start()

    depth = 256
    tile = 256

    def over_rows(first, second, shape):
        def piece(row):
            return lax.dot_general(
                first(row), second(row), (((0,), (0,)), ((), ())), preferred_element_type=jnp.float32)

        steps = nb * ROWS // depth
        if steps == 1:
            return piece(0)
        return lax.fori_loop(
            0, steps, lambda i, acc: acc + piece(pl.multiple_of(i * depth, depth)), jnp.zeros(shape, jnp.float32))

    def blocks(buf, row, col):
        return buf[pl.ds(row // ROWS, depth // ROWS), :, pl.ds(col, tile)].reshape(depth, tile)

    @pl.loop(0, width // tile)
    def _(i):
        col = pl.multiple_of(i * tile, tile)
        grad = over_rows(
            lambda row: blocks(x_all, row, col), lambda row: g_cat[pl.ds(row, depth), :], (tile, chunks * lat))
        enc_cat[pl.ds(col, tile), :] = (
            enc_cat[pl.ds(col, tile), :].astype(jnp.float32) - factor * grad).astype(jnp.bfloat16)

    stores = []
    for c in range(chunks):
        copy = pltpu.make_async_copy(
            enc_cat.at[:, pl.ds(c * lat, lat)], new_enc.at[pl.ds(c * width, width), :], local.at[2, c])
        copy.start()
        stores.append(copy)

    @pl.loop(0, width // tile)
    def _(i):
        col = pl.multiple_of(i * tile, tile)
        grad = over_rows(
            lambda row: e_cat[pl.ds(row, depth), :], lambda row: blocks(err_all, row, col), (chunks * lat, tile))
        dec_cat[:, pl.ds(col, tile)] = (
            dec_cat[:, pl.ds(col, tile)].astype(jnp.float32) - factor * grad).astype(jnp.bfloat16)

    for c in range(chunks):
        copy = pltpu.make_async_copy(
            dec_cat.at[pl.ds(c * lat, lat), :], new_dec.at[:, pl.ds(c * width, width)], local.at[3, c])
        copy.start()
        stores.append(copy)

    work_f[...] = err_all[0].astype(jnp.float32)

    @pl.loop(1, nb)
    def _(b):
        work_f[...] += err_all[b].astype(jnp.float32)

    total = term_send[...]

    def add_term(k, total):
        src = lax.rem(me + nl - k, nl)
        to_peer(term_send, term_recv.at[src], 10, k, src, src).wait_recv()
        return total + term_recv[src]

    total = lax.fori_loop(1, nl, add_term, total)
    per = 8 // chunks
    for c in range(chunks):
        sums = jnp.sum(work_f[c * t:(c + 1) * t, :], axis=0, keepdims=True)
        for h in range(per):
            r = c * per + h
            cols = slice(r * eighth, (r + 1) * eighth)
            new_dec_bias[:, cols] = dec_bias[:, cols] - factor * (
                sums[:, h * eighth:(h + 1) * eighth] - total[r:r + 1, :])

    gather_end(x_all, 0)
    gather_end(err_all, 6)

    @pl.loop(1, nl)
    def _(k):
        peer = lax.rem(me + k, nl)
        to_peer(r_send.at[peer], r_recv.at[me], 4, k, me, peer).wait_send()
        to_peer(term_send, term_recv.at[me], 10, k, me, peer).wait_send()

    for copy in stores:
        copy.wait()


def hand_on(*refs):
    count = (len(refs) - 1) // 3
    sems = refs[-1]
    loads, stores = [], []
    for i in range(count):
        src, dst, held = refs[i], refs[count + i], refs[2 * count + i]
        rows = src.shape[0]
        cuts = 4 if rows % 64 == 0 else 1
        for c in range(cuts):
            part = pl.ds(c * (rows // cuts), rows // cuts)
            loads.append(pltpu.make_async_copy(src.at[part], held.at[part], sems.at[0, i, c]))
            stores.append(pltpu.make_async_copy(held.at[part], dst.at[part], sems.at[1, i, c]))
    for load in loads:
        load.start()
    for load, store in zip(loads, stores):
        load.wait()
        store.start()
    for store in stores:
        store.wait()


def on_device(tokens, enc_weight, enc_bias, dec_weight, dec_bias):
    nl = lax.axis_size("latent")
    t, d = tokens.shape
    lat = enc_weight.shape[1]
    nb = 2 * nl
    chunks = ROWS // t
    width = d // chunks
    factor = STEP_RATE * 2.0 / (t * nb)
    scratch_bytes = (6 * nl + 2 * nb + 2 * ROWS) * ROWS * width * 2 + 4 * nb * ROWS * chunks * lat * 2 + nl * d * 4
    vmem = pl.BlockSpec(memory_space=pltpu.VMEM)
    anywhere = pl.BlockSpec(memory_space=pl.ANY)
    bf16, f32 = jnp.bfloat16, jnp.float32
    out = pl.pallas_call(
        functools.partial(kernel, nl, factor),
        out_shape=(
            jax.ShapeDtypeStruct((t, d), f32),
            jax.ShapeDtypeStruct((d, lat), bf16),
            jax.ShapeDtypeStruct((1, lat), f32),
            jax.ShapeDtypeStruct((lat, d), bf16),
            jax.ShapeDtypeStruct((1, d), f32),
        ),
        in_specs=[pl.BlockSpec(memory_space=pltpu.HBM)] * 5,
        out_specs=(vmem, anywhere, vmem, anywhere, vmem),
        scratch_shapes=[
            pltpu.VMEM((nb, ROWS, width), bf16),
            pltpu.VMEM((nb, ROWS, width), bf16),
            pltpu.VMEM((nl, ROWS, width), bf16),
            pltpu.VMEM((nl, ROWS, width), bf16),
            pltpu.VMEM((width, chunks * lat), bf16),
            pltpu.VMEM((chunks * lat, width), bf16),
            pltpu.VMEM((nb * ROWS, chunks * lat), bf16),
            pltpu.VMEM((nb * ROWS, chunks * lat), bf16),
            pltpu.VMEM((nb * ROWS, lat), bf16),
            pltpu.VMEM((ROWS, width), f32),
            pltpu.VMEM((ROWS, width), f32),
            pltpu.VMEM((ROWS, width), f32),
            pltpu.VMEM((8, lat), f32),
            pltpu.VMEM((8, d // 8), f32),
            pltpu.VMEM((nl, 8, d // 8), f32),
            pltpu.VMEM((t, d), bf16),
            pltpu.VMEM((1, lat), f32),
            pltpu.VMEM((1, d), f32),
            pltpu.SemaphoreType.DMA((12, nl)),
            pltpu.SemaphoreType.DMA((4, chunks)),
            pltpu.SemaphoreType.DMA((3,)),
        ],
        compiler_params=pltpu.CompilerParams(
            collective_id=0, has_side_effects=True, vmem_limit_bytes=60 * 1024 * 1024),
    )(tokens, enc_weight, enc_bias.reshape(1, lat), dec_weight, dec_bias.reshape(1, d))
    out = pl.pallas_call(
        hand_on,
        out_shape=tuple(jax.ShapeDtypeStruct(o.shape, o.dtype) for o in out),
        in_specs=[anywhere] * len(out),
        out_specs=(anywhere,) * len(out),
        scratch_shapes=[pltpu.VMEM(o.shape, o.dtype) for o in out] + [pltpu.SemaphoreType.DMA((2, len(out), 4))],
        compiler_params=pltpu.CompilerParams(vmem_limit_bytes=60 * 1024 * 1024),
    )(*out)
    recon, new_enc, new_enc_bias, new_dec, new_dec_bias = out
    return recon, new_enc, new_enc_bias.reshape(lat), new_dec, new_dec_bias.reshape(d)


def solution(mesh):
    specs = (
        P(("group", "latent", "dp"), None),
        P("group", "latent"),
        P(("group", "latent")),
        P(("group", "latent"), None),
        P("group"),
    )
    return jax.shard_map(on_device, mesh=mesh, in_specs=specs, out_specs=specs, check_vma=False)
```

```python
import functools

import jax
import jax.numpy as jnp
from jax import lax
from jax.experimental import pallas as pl
from jax.experimental.pallas import tpu as pltpu
from jax.sharding import PartitionSpec as P

STEP_RATE = 0.1
MESH = pl.DeviceIdType.MESH
ROWS = 16


def kernel(
    nl, factor,
    tokens_hbm, enc_hbm, enc_bias_hbm, dec_hbm, dec_bias_hbm,
    recon_out, new_enc, new_enc_bias, new_dec, new_dec_bias,
    x_all, err_all, r_send, r_recv, enc_cat, dec_cat, e_cat, g_cat, codes_all,
    tok_f, bias_f, work_f, rates, term_send, term_recv, tokens, enc_bias, dec_bias, sems, local, small,
):
    me = lax.axis_index("latent")
    slab = lax.axis_index("dp")
    t, d = tokens.shape
    chunks = ROWS // t
    width = d // chunks
    lat = enc_bias.shape[1]
    nb = 2 * nl
    mine = slab * nl
    other = (1 - slab) * nl

    barrier = pltpu.get_barrier_semaphore()

    @pl.loop(1, nl)
    def _(k):
        pl.semaphore_signal(barrier, inc=1, device_id={"latent": lax.rem(me + k, nl)}, device_id_type=MESH)

    pl.semaphore_signal(barrier, inc=1, device_id={"dp": 1 - slab}, device_id_type=MESH)

    first_loads = [
        pltpu.make_async_copy(src, dst, small.at[i])
        for i, (src, dst) in enumerate(((tokens_hbm, tokens), (dec_bias_hbm, dec_bias), (enc_bias_hbm, enc_bias)))]
    for copy in first_loads:
        copy.start()
    loads = []
    for c in range(chunks):
        loads.append(pltpu.make_async_copy(
            enc_hbm.at[pl.ds(c * width, width), :], enc_cat.at[:, pl.ds(c * lat, lat)], local.at[0, c]))
    for c in range(chunks):
        loads.append(pltpu.make_async_copy(
            dec_hbm.at[:, pl.ds(c * width, width)], dec_cat.at[pl.ds(c * lat, lat), :], local.at[1, c]))
    for copy in loads:
        copy.start()

    for copy in first_loads:
        copy.wait()
    for c in range(chunks):
        tok_f[c * t:(c + 1) * t, :] = tokens[:, c * width:(c + 1) * width].astype(jnp.float32)
        bias_f[c * t:(c + 1) * t, :] = jnp.broadcast_to(dec_bias[:, c * width:(c + 1) * width], (t, width))
    x_all[mine + me] = (tok_f[...] - bias_f[...]).astype(jnp.bfloat16)
    pl.semaphore_wait(barrier, nl)

    def to_peer(src, dst, kind, send, recv, peer):
        return pltpu.make_async_remote_copy(
            src_ref=src, dst_ref=dst, send_sem=sems.at[kind, send], recv_sem=sems.at[kind + 1, recv],
            device_id={"latent": peer}, device_id_type=MESH)

    def to_partner(buf, kind, block):
        return pltpu.make_async_remote_copy(
            src_ref=buf.at[mine + block], dst_ref=buf.at[mine + block],
            send_sem=sems.at[kind, block], recv_sem=sems.at[kind + 1, block],
            device_id={"dp": 1 - slab}, device_id_type=MESH)

    pair = me + 1 - 2 * lax.rem(me, 2)

    def gather_start(buf, kind):
        to_peer(buf.at[mine + me], buf.at[mine + me], kind, 0, me, pair).start()

        @pl.loop(1, nl // 2)
        def _(k):
            to_peer(buf.at[mine + me], buf.at[mine + me], kind, k, me, lax.rem(me + 2 * k, nl)).start()

        to_partner(buf, kind + 2, me).start()

    def gather_forward(buf, kind):
        def arrived(src):
            to_peer(buf.at[mine + src], buf.at[mine + src], kind, 0, src, src).wait_recv()

        @pl.loop(1, nl // 2)
        def _(k):
            src = lax.rem(me + nl - 2 * k, nl)
            arrived(src)
            to_peer(buf.at[mine + src], buf.at[mine + src], kind, nl // 2 + k, src, pair).start()
            to_partner(buf, kind + 2, src).start()

        @pl.loop(0, nl // 2)
        def _(k):
            src = lax.rem(pair + nl - 2 * k, nl)
            arrived(src)
            to_partner(buf, kind + 2, src).start()

    def gather_other(buf, kind):
        @pl.loop(0, nl)
        def _(j):
            pltpu.make_async_remote_copy(
                src_ref=buf.at[other + j], dst_ref=buf.at[other + j],
                send_sem=sems.at[kind + 2, j], recv_sem=sems.at[kind + 3, j],
                device_id={"dp": 1 - slab}, device_id_type=MESH).wait_recv()

    def gather_end(buf, kind):
        @pl.loop(1, nl // 2)
        def _(k):
            to_peer(buf.at[mine + me], buf.at[mine + me], kind, k, me, pair).wait_send()
            to_peer(buf.at[mine + me], buf.at[mine + me], kind, nl // 2 + k, me, pair).wait_send()

        to_peer(buf.at[mine + me], buf.at[mine + me], kind, 0, me, pair).wait_send()

        @pl.loop(0, nl)
        def _(j):
            to_partner(buf, kind + 2, j).wait_send()

    group = 8
    span = group * ROWS
    chunk_of = lax.rem(lax.broadcasted_iota(jnp.int32, (span, lat), 0), ROWS) // t

    def fold(value):
        picked = value[:, :lat]
        for c in range(1, chunks):
            picked = jnp.where(chunk_of == c, value[:, c * lat:(c + 1) * lat], picked)
        picked = picked.reshape(group, ROWS, lat)
        half = picked[:, :8] + picked[:, 8:]
        shift = 4
        while shift >= t:
            half = half + pltpu.roll(half, shift, 1)
            shift //= 2
        return jnp.concatenate([half, half], axis=1).reshape(span, lat)

    def spread(value, dst, row):
        for c in range(chunks):
            dst[pl.ds(row, span), c * lat:(c + 1) * lat] = jnp.where(chunk_of == c, value, 0.0).astype(jnp.bfloat16)

    def encode(first):
        @pl.loop(0, nl // group)
        def _(g):
            block = first + g * group
            row = pl.multiple_of(block * ROWS, span)
            x = x_all[pl.ds(block, group)].reshape(span, width)
            pre = fold(jnp.dot(x, enc_cat[...], preferred_element_type=jnp.float32)) + enc_bias[...]
            codes = jnp.maximum(pre, 0.0).astype(jnp.bfloat16)
            codes_all[pl.ds(row, span), :] = codes
            spread(codes.astype(jnp.float32), e_cat, row)

    gather_start(x_all, 0)
    for c in range(chunks):
        loads[c].wait()
    gather_forward(x_all, 0)
    encode(mine)
    for c in range(chunks):
        loads[chunks + c].wait()

    @pl.loop(0, nl // group)
    def _(g):
        row = pl.multiple_of((mine + g * group) * ROWS, span)
        part = jnp.dot(e_cat[pl.ds(row, span), :], dec_cat[...], preferred_element_type=jnp.float32)
        r_send[pl.ds(g * group, group)] = part.astype(jnp.bfloat16).reshape(group, ROWS, width)

    @pl.loop(1, nl)
    def _(k):
        peer = lax.rem(me + k, nl)
        to_peer(r_send.at[peer], r_recv.at[me], 4, k, me, peer).start()

    gather_other(x_all, 0)
    encode(other)

    work_f[...] = r_send[me].astype(jnp.float32) + bias_f[...]

    @pl.loop(1, nl)
    def _(k):
        src = lax.rem(me + nl - k, nl)
        to_peer(r_send.at[src], r_recv.at[src], 4, k, src, src).wait_recv()
        work_f[...] += r_recv[src].astype(jnp.float32)

    err_all[mine + me] = (work_f[...] - tok_f[...]).astype(jnp.bfloat16)
    gather_start(err_all, 6)
    for c in range(chunks):
        recon_out[:, c * width:(c + 1) * width] = work_f[c * t:(c + 1) * t, :]
    gather_forward(err_all, 6)

    def backward(first, which):
        rates[which:which + 1, :] = jnp.zeros((1, lat), jnp.float32)

        @pl.loop(0, nl // group)
        def _(g):
            block = first + g * group
            row = pl.multiple_of(block * ROWS, span)
            err = err_all[pl.ds(block, group)].reshape(span, width)
            back = fold(lax.dot_general(
                err, dec_cat[...], (((1,), (1,)), ((), ())), preferred_element_type=jnp.float32))
            kept = codes_all[pl.ds(row, span), :].astype(jnp.float32) > 0
            grad = jnp.where(kept, back, 0.0).astype(jnp.bfloat16).astype(jnp.float32)
            spread(grad, g_cat, row)
            rates[which:which + 1, :] += jnp.sum(jnp.where(chunk_of == 0, grad, 0.0), axis=0, keepdims=True)

    backward(mine, 0)
    gather_other(err_all, 6)
    backward(other, 1)

    rate_0, rate_1 = rates[0:1, :], rates[1:2, :]
    new_enc_bias[...] = enc_bias[...] - factor * (
        rate_0.astype(jnp.bfloat16).astype(jnp.float32) + rate_1.astype(jnp.bfloat16).astype(jnp.float32))
    rate = rate_0 + rate_1
    high = rate.astype(jnp.bfloat16).astype(jnp.float32)
    mid = (rate - high).astype(jnp.bfloat16).astype(jnp.float32)
    low = rate - high - mid
    index = lax.broadcasted_iota(jnp.int32, (16, lat), 0)
    pieces = jnp.where(index == 0, high, jnp.where(index == 1, mid, jnp.where(index == 2, low, 0.0)))
    pieces = pieces.astype(jnp.bfloat16)
    eighth = d // 8
    for c in range(chunks):
        term = jnp.sum(lax.dot_general(
            pieces, enc_cat[:, c * lat:(c + 1) * lat], (((1,), (1,)), ((), ())),
            preferred_element_type=jnp.float32), axis=0, keepdims=True)
        for h in range(8 // chunks):
            r = c * (8 // chunks) + h
            term_send[r:r + 1, :] = term[:, h * eighth:(h + 1) * eighth]

    @pl.loop(1, nl)
    def _(k):
        to_peer(term_send, term_recv.at[me], 10, k, me, lax.rem(me + k, nl)).start()

    depth = 256
    tile = 256

    def over_rows(first, second, shape):
        def piece(row):
            return lax.dot_general(
                first(row), second(row), (((0,), (0,)), ((), ())), preferred_element_type=jnp.float32)

        steps = nb * ROWS // depth
        if steps == 1:
            return piece(0)
        return lax.fori_loop(
            0, steps, lambda i, acc: acc + piece(pl.multiple_of(i * depth, depth)), jnp.zeros(shape, jnp.float32))

    def blocks(buf, row, col):
        return buf[pl.ds(row // ROWS, depth // ROWS), :, pl.ds(col, tile)].reshape(depth, tile)

    @pl.loop(0, width // tile)
    def _(i):
        col = pl.multiple_of(i * tile, tile)
        grad = over_rows(
            lambda row: blocks(x_all, row, col), lambda row: g_cat[pl.ds(row, depth), :], (tile, chunks * lat))
        enc_cat[pl.ds(col, tile), :] = (
            enc_cat[pl.ds(col, tile), :].astype(jnp.float32) - factor * grad).astype(jnp.bfloat16)

    stores = []
    for c in range(chunks):
        copy = pltpu.make_async_copy(
            enc_cat.at[:, pl.ds(c * lat, lat)], new_enc.at[pl.ds(c * width, width), :], local.at[2, c])
        copy.start()
        stores.append(copy)

    @pl.loop(0, width // tile)
    def _(i):
        col = pl.multiple_of(i * tile, tile)
        grad = over_rows(
            lambda row: e_cat[pl.ds(row, depth), :], lambda row: blocks(err_all, row, col), (chunks * lat, tile))
        dec_cat[:, pl.ds(col, tile)] = (
            dec_cat[:, pl.ds(col, tile)].astype(jnp.float32) - factor * grad).astype(jnp.bfloat16)

    for c in range(chunks):
        copy = pltpu.make_async_copy(
            dec_cat.at[pl.ds(c * lat, lat), :], new_dec.at[:, pl.ds(c * width, width)], local.at[3, c])
        copy.start()
        stores.append(copy)

    work_f[...] = err_all[0].astype(jnp.float32)

    @pl.loop(1, nb)
    def _(b):
        work_f[...] += err_all[b].astype(jnp.float32)

    total = term_send[...]

    def add_term(k, total):
        src = lax.rem(me + nl - k, nl)
        to_peer(term_send, term_recv.at[src], 10, k, src, src).wait_recv()
        return total + term_recv[src]

    total = lax.fori_loop(1, nl, add_term, total)
    per = 8 // chunks
    for c in range(chunks):
        sums = jnp.sum(work_f[c * t:(c + 1) * t, :], axis=0, keepdims=True)
        for h in range(per):
            r = c * per + h
            cols = slice(r * eighth, (r + 1) * eighth)
            new_dec_bias[:, cols] = dec_bias[:, cols] - factor * (
                sums[:, h * eighth:(h + 1) * eighth] - total[r:r + 1, :])

    gather_end(x_all, 0)
    gather_end(err_all, 6)

    @pl.loop(1, nl)
    def _(k):
        peer = lax.rem(me + k, nl)
        to_peer(r_send.at[peer], r_recv.at[me], 4, k, me, peer).wait_send()
        to_peer(term_send, term_recv.at[me], 10, k, me, peer).wait_send()

    for copy in stores:
        copy.wait()


def hand_on(*refs):
    count = (len(refs) - 1) // 3
    sems = refs[-1]
    loads, stores = [], []
    for i in range(count):
        src, dst, held = refs[i], refs[count + i], refs[2 * count + i]
        rows = src.shape[0]
        cuts = 4 if rows % 64 == 0 else 1
        for c in range(cuts):
            part = pl.ds(c * (rows // cuts), rows // cuts)
            loads.append(pltpu.make_async_copy(src.at[part], held.at[part], sems.at[0, i, c]))
            stores.append(pltpu.make_async_copy(held.at[part], dst.at[part], sems.at[1, i, c]))
    for load in loads:
        load.start()
    for load, store in zip(loads, stores):
        load.wait()
        store.start()
    for store in stores:
        store.wait()


def on_device(tokens, enc_weight, enc_bias, dec_weight, dec_bias):
    nl = lax.axis_size("latent")
    t, d = tokens.shape
    lat = enc_weight.shape[1]
    nb = 2 * nl
    chunks = ROWS // t
    width = d // chunks
    factor = STEP_RATE * 2.0 / (t * nb)
    scratch_bytes = (6 * nl + 2 * nb + 2 * ROWS) * ROWS * width * 2 + 4 * nb * ROWS * chunks * lat * 2 + nl * d * 4
    vmem = pl.BlockSpec(memory_space=pltpu.VMEM)
    anywhere = pl.BlockSpec(memory_space=pl.ANY)
    bf16, f32 = jnp.bfloat16, jnp.float32
    out = pl.pallas_call(
        functools.partial(kernel, nl, factor),
        out_shape=(
            jax.ShapeDtypeStruct((t, d), f32),
            jax.ShapeDtypeStruct((d, lat), bf16),
            jax.ShapeDtypeStruct((1, lat), f32),
            jax.ShapeDtypeStruct((lat, d), bf16),
            jax.ShapeDtypeStruct((1, d), f32),
        ),
        in_specs=[pl.BlockSpec(memory_space=pltpu.HBM)] * 5,
        out_specs=(vmem, anywhere, vmem, anywhere, vmem),
        scratch_shapes=[
            pltpu.VMEM((nb, ROWS, width), bf16),
            pltpu.VMEM((nb, ROWS, width), bf16),
            pltpu.VMEM((nl, ROWS, width), bf16),
            pltpu.VMEM((nl, ROWS, width), bf16),
            pltpu.VMEM((width, chunks * lat), bf16),
            pltpu.VMEM((chunks * lat, width), bf16),
            pltpu.VMEM((nb * ROWS, chunks * lat), bf16),
            pltpu.VMEM((nb * ROWS, chunks * lat), bf16),
            pltpu.VMEM((nb * ROWS, lat), bf16),
            pltpu.VMEM((ROWS, width), f32),
            pltpu.VMEM((ROWS, width), f32),
            pltpu.VMEM((ROWS, width), f32),
            pltpu.VMEM((8, lat), f32),
            pltpu.VMEM((8, d // 8), f32),
            pltpu.VMEM((nl, 8, d // 8), f32),
            pltpu.VMEM((t, d), bf16),
            pltpu.VMEM((1, lat), f32),
            pltpu.VMEM((1, d), f32),
            pltpu.SemaphoreType.DMA((12, nl)),
            pltpu.SemaphoreType.DMA((4, chunks)),
            pltpu.SemaphoreType.DMA((3,)),
        ],
        compiler_params=pltpu.CompilerParams(
            collective_id=0, has_side_effects=True, vmem_limit_bytes=60 * 1024 * 1024),
    )(tokens, enc_weight, enc_bias.reshape(1, lat), dec_weight, dec_bias.reshape(1, d))
    out = pl.pallas_call(
        hand_on,
        out_shape=tuple(jax.ShapeDtypeStruct(o.shape, o.dtype) for o in out),
        in_specs=[anywhere] * len(out),
        out_specs=(anywhere,) * len(out),
        scratch_shapes=[pltpu.VMEM(o.shape, o.dtype) for o in out] + [pltpu.SemaphoreType.DMA((2, len(out), 4))],
        compiler_params=pltpu.CompilerParams(vmem_limit_bytes=60 * 1024 * 1024),
    )(*out)
    recon, new_enc, new_enc_bias, new_dec, new_dec_bias = out
    return recon, new_enc, new_enc_bias.reshape(lat), new_dec, new_dec_bias.reshape(d)


def solution(mesh):
    specs = (
        P(("group", "latent", "dp"), None),
        P("group", "latent"),
        P(("group", "latent")),
        P(("group", "latent"), None),
        P("group"),
    )
    return jax.shard_map(on_device, mesh=mesh, in_specs=specs, out_specs=specs, check_vma=False)
```
